256 devices in a mesh: row: 16 (over z, core), col: 8 (over y_hi, x), depth: 2 (over y_lo).
Axes of the slice: x: 4, y: 4 (y_hi: 2, y_lo: 2; y = y_hi * 2 + y_lo), z: 8, core: 2. Of those that a mesh axis runs over, the one named last changes fastest.
Arguments:
- inputs: bfloat16 [1024, 6144], P(('depth', 'col'), 'row'), may hold values from -6 to 6
- cotangent: bfloat16 [1024, 6144], P(('depth', 'col'), 'row'), may hold values from -1.5 to 1.5
- w_in: bfloat16 [6144, 24576], P('row', 'col'), may hold values from -0.078125 to 0.078125
- w_out: bfloat16 [24576, 6144], P('col', 'row'), may hold values from -0.0390625 to 0.0390625
Outputs:
- outputs: bfloat16 [1024, 6144], P(('depth', 'col'), 'row')
- grad_inputs: bfloat16 [1024, 6144], P(('depth', 'col'), 'row')
- grad_w_in: bfloat16 [6144, 24576], P('row', ('col', 'depth'))
- grad_w_out: bfloat16 [24576, 6144], P('col', ('row', 'depth'))
The draws below stay inside these ranges and needn't reach their ends.
All inputs are finite; a program needn't handle non-finite values.
Results may differ from the reference program's by a relative error of at most 0.03.
Values may be sent and summed in bfloat16 or wider, within the bound.
No kernel may reach another device: no remote copies, remote signals or barrier semaphores. Data moves between devices by JAX's collectives and lax.ppermute only.
A program may use at most 64 MiB of HBM per device.

```python
import jax
import jax.numpy as jnp
from jax import lax

D = 6144
FF = 24576
GROUP_TOKENS = 512
TOKENS = 1024
N_ROW = 16
N_DEPTH = 2


def steps_of(key, dims, pieces, low, high):
    def one(position, parts):
        steps = jax.random.uniform(jax.random.fold_in(jax.random.fold_in(key, 6), position), (parts,), jnp.float32, low / len(pieces), high / len(pieces))
        return jnp.repeat(jnp.exp(steps), dims[position] // parts).reshape((-1,) + (1,) * (len(dims) - position - 1))

    loudness = one(*pieces[0])
    for cut in pieces[1:]:
        loudness = loudness * one(*cut)
    return loudness


def gaussian(stream_key, dims, width, limit, cuts=(), held_as=jnp.bfloat16):
    entries = width * jax.random.normal(stream_key, dims, jnp.float32)
    if cuts:
        entries = entries * steps_of(stream_key, dims, cuts, -0.22, 0.18)
    return jnp.clip(entries, -limit, limit).astype(held_as)


def setup_inputs(seed: int = 0) -> dict:
    streams_of = jax.random.split(jax.random.key(seed), 5)
    inputs = gaussian(streams_of[0], (TOKENS, D), 1.0, 6.0, ((0, 16), (1, 16)))
    cotangent = gaussian(streams_of[1], (TOKENS, D), 0.25, 1.5, ((0, 16), (1, 16)))
    w_in = gaussian(streams_of[2], (D, FF), D ** -0.5, 0.078125, ((0, 16), (1, 8)))
    w_out = gaussian(streams_of[3], (FF, D), FF ** -0.5, 0.0390625, ((0, 8), (1, 16)))
    return {"inputs": inputs, "cotangent": cotangent, "w_in": w_in, "w_out": w_out}


gelu_c = 0.7978845608028654
gelu_k = 0.044715


def gelu_pair(preact):
    inner = gelu_c * (preact + gelu_k * preact * preact * preact)
    tangent = jnp.tanh(inner)
    gelu_value = 0.5 * preact * (1.0 + tangent)
    gelu_slope = 0.5 * (1.0 + tangent) + 0.5 * preact * (1.0 - tangent * tangent) * gelu_c * (1.0 + 3.0 * gelu_k * preact * preact)
    return gelu_value, gelu_slope


def round_trip(values):
    return lax.optimization_barrier(values.astype(jnp.bfloat16)).astype(jnp.float32)


def reference(inputs, cotangent, w_in, w_out):
    blocks = D // N_ROW

    def add_pre(index, carry):
        offset = (index * blocks).astype(jnp.int32)
        left = lax.dynamic_slice_in_dim(inputs, offset, blocks, 1)
        right = lax.dynamic_slice_in_dim(w_in, offset, blocks, 0)
        return carry + round_trip(jnp.dot(left, right, preferred_element_type=jnp.float32))

    preact = lax.fori_loop(0, N_ROW, add_pre, jnp.zeros((TOKENS, FF), jnp.float32))
    gelu_value, gelu_slope = gelu_pair(preact)
    hidden = gelu_value.astype(jnp.bfloat16)
    outputs = jnp.dot(hidden, w_out, preferred_element_type=jnp.float32).astype(jnp.bfloat16)

    def add_back(index, carry):
        offset = (index * blocks).astype(jnp.int32)
        left = lax.dynamic_slice_in_dim(cotangent, offset, blocks, 1)
        right = lax.dynamic_slice_in_dim(w_out, offset, blocks, 1)
        term = lax.dot_general(left, right, (((1,), (1,)), ((), ())), preferred_element_type=jnp.float32)
        return carry + round_trip(term)

    grad_hidden = lax.fori_loop(0, N_ROW, add_back, jnp.zeros((TOKENS, FF), jnp.float32)).astype(jnp.bfloat16)
    grad_pre = (grad_hidden.astype(jnp.float32) * gelu_slope).astype(jnp.bfloat16)
    grad_inputs = lax.dot_general(grad_pre, w_in, (((1,), (1,)), ((), ())), preferred_element_type=jnp.float32).astype(jnp.bfloat16)
    grad_w_out = jnp.zeros((FF, D), jnp.float32)
    grad_w_in = jnp.zeros((D, FF), jnp.float32)
    for group in range(N_DEPTH):
        first_row = group * GROUP_TOKENS
        hidden_part = hidden[first_row:first_row + GROUP_TOKENS]
        cot_part = cotangent[first_row:first_row + GROUP_TOKENS]
        input_part = inputs[first_row:first_row + GROUP_TOKENS]
        slope_part = grad_pre[first_row:first_row + GROUP_TOKENS]
        grad_w_out = grad_w_out + round_trip(lax.dot_general(hidden_part, cot_part, (((0,), (0,)), ((), ())), preferred_element_type=jnp.float32))
        grad_w_in = grad_w_in + round_trip(lax.dot_general(input_part, slope_part, (((0,), (0,)), ((), ())), preferred_element_type=jnp.float32))
    return outputs, grad_inputs, grad_w_in.astype(jnp.bfloat16), grad_w_out.astype(jnp.bfloat16)
```

```python
import jax
import jax.numpy as jnp
from jax import lax
from jax.sharding import Mesh
from jax.sharding import PartitionSpec as P

gelu_c = 0.7978845608028654
gelu_k = 0.044715

NZ = 8
PLANE = ("yl", "yh", "x")
f32 = jnp.float32
bf16 = jnp.bfloat16

UP = [(i, (i + 1) % NZ) for i in range(NZ)]
DOWN = [(i, (i - 1) % NZ) for i in range(NZ)]
SWAP = [(0, 1), (1, 0)]


def gelu_pair(preact):
    inner = gelu_c * (preact + gelu_k * preact * preact * preact)
    tangent = jnp.tanh(inner)
    gelu_value = 0.5 * preact * (1.0 + tangent)
    gelu_slope = 0.5 * (1.0 + tangent) + 0.5 * preact * (1.0 - tangent * tangent) * gelu_c * (
        1.0 + 3.0 * gelu_k * preact * preact
    )
    return (gelu_value, gelu_slope)


def up(v):
    return lax.ppermute(v, "z", UP)


def down(v):
    return lax.ppermute(v, "z", DOWN)


def swap_core(v):
    return lax.ppermute(v, "core", SWAP)


def dot(a, b, ca, cb):
    return lax.dot_general(a, b, (((ca,), (cb,)), ((), ())), preferred_element_type=f32)


def reduce_ring(partial, z):
    rows = partial.shape[0] // NZ
    half = partial.shape[1] // 2

    def chunk(k):
        return lax.dynamic_slice_in_dim(partial, ((z + k) % NZ) * rows, rows, 0)

    far = chunk(4)
    from_below = up(far[:, :half].astype(bf16)).astype(f32)
    from_above = down(far[:, half:].astype(bf16)).astype(f32)
    nxt_up, nxt_down = chunk(3), chunk(5)
    send_up = jnp.concatenate([nxt_up[:, :half] + from_below, nxt_up[:, half:]], 1)
    send_down = jnp.concatenate([nxt_down[:, :half], nxt_down[:, half:] + from_above], 1)
    for k in (2, 1, 0):
        from_below = up(send_up.astype(bf16)).astype(f32)
        from_above = down(send_down.astype(bf16)).astype(f32)
        if k:
            send_up = chunk(k) + from_below
            send_down = chunk(NZ - k) + from_above
    return chunk(0) + from_below + from_above


def gather_ring(own, z):
    rows, width = own.shape
    half = width // 2
    whole = jnp.zeros((NZ * rows, width), own.dtype)

    def put(whole, block, k, column=0):
        return lax.dynamic_update_slice(whole, block, (((z + k) % NZ) * rows, column))

    whole = put(whole, own, 0)
    go_up = go_down = own
    for k in (1, 2, 3):
        go_up, go_down = up(go_up), down(go_down)
        whole = put(whole, go_up, NZ - k)
        whole = put(whole, go_down, k)
    whole = put(whole, up(go_up[:, :half]), 4)
    whole = put(whole, down(go_down[:, half:]), 4, half)
    return whole


def on_device(inputs, cotangent, w_in, w_out):
    z, core, yl = lax.axis_index("z"), lax.axis_index("core"), lax.axis_index("yl")
    width = inputs.shape[1]
    units = w_in.shape[1] // 4
    mine = (yl * 2 + core) * units
    theirs = (yl * 2 + 1 - core) * units

    w_in_other = swap_core(lax.dynamic_slice_in_dim(w_in, theirs, units, 1))
    w_out_other = swap_core(lax.dynamic_slice_in_dim(w_out, theirs, units, 0))
    w_in_own = lax.dynamic_slice_in_dim(w_in, mine, units, 1)
    w_out_own = lax.dynamic_slice_in_dim(w_out, mine, units, 0)

    both = jnp.concatenate([inputs, cotangent], 1)
    both_all = lax.all_to_all(
        jnp.broadcast_to(both[None], (16,) + both.shape).reshape(-1, both.shape[1]),
        PLANE, 0, 0, tiled=True,
    )
    both_other = swap_core(both_all)
    x_own, dy_own = both_all[:, :width], both_all[:, width:]
    x_other, dy_other = both_other[:, :width], both_other[:, width:]
    x = jnp.concatenate([x_own, x_other], 1)
    dy = jnp.concatenate([dy_own, dy_other], 1)
    w_i = jnp.concatenate([w_in_own, w_in_other], 0)
    w_o = jnp.concatenate([w_out_own, w_out_other], 1)

    preact = reduce_ring(dot(x, w_i, 1, 0), z)
    grad_hidden = reduce_ring(dot(dy, w_o, 1, 1), z).astype(bf16)
    gelu_value, gelu_slope = gelu_pair(preact)
    hidden = gather_ring(gelu_value.astype(bf16), z)
    grad_pre = gather_ring((grad_hidden.astype(f32) * gelu_slope).astype(bf16), z)

    quarter = width // 2

    def w_out_block(part, which):
        columns = lax.dynamic_slice_in_dim(part, which * quarter, quarter, 1)
        return dot(hidden, columns, 0, 0).astype(bf16)

    pair = ("core", "yl")
    flip_yl = [(i, i ^ 1) for i in range(4)]
    flip_both = [(i, i ^ 3) for i in range(4)]
    blocks = (
        (yl, core, w_out_block(dy_own, yl)),
        (yl, 1 - core, swap_core(w_out_block(dy_other, yl))),
        (1 - yl, core, lax.ppermute(w_out_block(dy_own, 1 - yl), pair, flip_yl)),
        (1 - yl, 1 - core, lax.ppermute(w_out_block(dy_other, 1 - yl), pair, flip_both)),
    )
    grad_w_out = jnp.zeros((4 * units, quarter), bf16)
    for src_yl, src_core, block in blocks:
        grad_w_out = lax.dynamic_update_slice(grad_w_out, block, ((src_yl * 2 + src_core) * units, 0))

    out_sent = swap_core(dot(hidden, w_out_other, 1, 0).astype(bf16))
    gin_sent = swap_core(dot(grad_pre, w_in_other, 1, 1).astype(bf16))
    out_part = (dot(hidden, w_out_own, 1, 0) + out_sent.astype(f32)).astype(bf16)
    gin_part = (dot(grad_pre, w_in_own, 1, 1) + gin_sent.astype(f32)).astype(bf16)

    gwi_sent = swap_core(dot(x_other, grad_pre, 0, 0).astype(bf16))
    gwi_own = dot(x_own, grad_pre, 0, 0).astype(bf16)
    grad_w_in = jnp.zeros((width, 2 * units), bf16)
    grad_w_in = lax.dynamic_update_slice(grad_w_in, gwi_own, (0, core * units))
    grad_w_in = lax.dynamic_update_slice(grad_w_in, gwi_sent, (0, (1 - core) * units))

    parts = lax.all_to_all(jnp.concatenate([out_part, gin_part], 1), PLANE, 0, 0, tiled=True)
    total = parts.reshape(16, -1, 2 * width).astype(f32).sum(0).astype(bf16)
    return total[:, :width], total[:, width:], grad_w_in, grad_w_out


def solution(mesh):
    grid = Mesh(mesh.devices.reshape(NZ, 2, 2, 4, 2), ("z", "core", "yh", "x", "yl"))
    row, col = ("z", "core"), ("yh", "x")
    in_specs = (P(PLANE, row), P(PLANE, row), P(row, col), P(col, row))
    out_specs = (P(PLANE, row), P(PLANE, row), P(row, col + ("yl",)), P(col, row + ("yl",)))
    return jax.shard_map(
        on_device, mesh=grid, in_specs=in_specs, out_specs=out_specs, check_vma=False
    )
```

```python
import functools
import math

import jax
import jax.numpy as jnp
from jax import lax
from jax.experimental import pallas as pl
from jax.experimental.pallas import tpu as pltpu
from jax.sharding import Mesh
from jax.sharding import PartitionSpec as P

gelu_c = 0.7978845608028654
gelu_k = 0.044715

NZ = 8
NP = 16
PLANE = ("yl", "yh", "x")
f32 = jnp.float32
bf16 = jnp.bfloat16

UP = [(i, (i + 1) % NZ) for i in range(NZ)]
DOWN = [(i, (i - 1) % NZ) for i in range(NZ)]
SWAP = [(0, 1), (1, 0)]

Z, CORE, YL, MINE, THEIRS = range(5)


def gelu_pair(preact):
    inner = gelu_c * (preact + gelu_k * preact * preact * preact)
    tangent = jnp.tanh(inner)
    gelu_value = 0.5 * preact * (1.0 + tangent)
    gelu_slope = 0.5 * (1.0 + tangent) + 0.5 * preact * (1.0 - tangent * tangent) * gelu_c * (
        1.0 + 3.0 * gelu_k * preact * preact
    )
    return (gelu_value, gelu_slope)


def up(v):
    return lax.ppermute(v, "z", UP)


def down(v):
    return lax.ppermute(v, "z", DOWN)


def swap_core(v):
    return lax.ppermute(v, "core", SWAP)


def plane_swap(v):
    return lax.all_to_all(v, PLANE, 0, 0, tiled=True)


def dot(a, b, ca, cb):
    return lax.dot_general(a, b, (((ca,), (cb,)), ((), ())), preferred_element_type=f32)


def in_hbm(v):
    return pltpu.with_memory_space_constraint(v, pltpu.HBM)


def whole(shape):
    return pl.BlockSpec(shape, lambda i, s: (0,) * len(shape), pipeline_mode=pl.Buffered(1))


def call(body, scalars, args, specs, outs, flops=0, after=(), out_specs=None, steps=1, touched=None, scratch=()):
    in_specs = [whole(a.shape) if s is None else s for a, s in zip(args, specs)]
    in_specs += [pl.BlockSpec(memory_space=pl.ANY)] * len(after)
    n = len(args)

    def run(s, *refs):
        body(s, *refs[:n], *refs[n + len(after):])

    if touched is None:
        touched = sum(a.size * a.dtype.itemsize for a in args) + sum(2 * math.prod(o.shape) for o in outs)
    return pl.pallas_call(
        run,
        out_shape=outs,
        grid_spec=pltpu.PrefetchScalarGridSpec(
            num_scalar_prefetch=1,
            grid=(steps,),
            in_specs=in_specs,
            scratch_shapes=scratch,
            out_specs=out_specs or [pl.BlockSpec(o.shape, lambda i, s: (0, 0)) for o in outs],
        ),
        compiler_params=pltpu.CompilerParams(vmem_limit_bytes=16 * 1024 * 1024),
        cost_estimate=pl.CostEstimate(flops=flops, bytes_accessed=touched, transcendentals=0),
    )(scalars, *args, *after)


def sds(shape, dtype=bf16):
    return jax.ShapeDtypeStruct(shape, dtype)


def spread_kernel(s, x, dy, spread):
    rows = x.shape[0]
    both = jnp.concatenate([x[...], dy[...]], 1)
    for p in range(NP):
        spread[pl.ds(p * rows, rows), :] = both


def copy_kernel(s, w_in, w_out, w_in_send, w_out_send):
    w_in_send[...] = w_in[...]
    w_out_send[...] = w_out[...]


def arrange_kernel(s, w_in, w_in_other, w_out, w_out_other, wi_turned, wo, wo_turned):
    width = w_in.shape[0]
    for side, (i, o) in enumerate(((w_in, w_out), (w_in_other, w_out_other))):
        part = pl.ds(side * width, width)
        wi_turned[:, part] = i[...].T
        wo[:, part] = o[...]
        wo_turned[part, :] = o[...].T


def chunk_rows(index, rows):
    return pl.ds(pl.multiple_of(index * rows, rows), rows)


def partial_kernel(s, own, other, weight, out, send_up, send_down):
    rows, half = send_up.shape
    z = s[Z]
    width = weight.shape[0] // 2
    for t in range(NZ // 2):
        tokens = pl.ds(t * 2 * rows, 2 * rows)
        left = jnp.concatenate([own[tokens, width:], other[tokens, width:]], 1)
        acc = dot(left, weight[...], 1, 0).astype(bf16)
        for c in range(2):
            place = lax.rem(2 * t + c - z + NZ, NZ)
            out[chunk_rows(place, rows), :] = acc[c * rows:(c + 1) * rows]
    send_up[...] = out[pl.ds(4 * rows, rows), :half]
    send_down[...] = out[pl.ds(4 * rows, rows), half:]


def own_half_kernel(s, own, weight, out):
    for t in range(4):
        part = pl.ds(t * 256, 256)
        out[part, :] = dot(own[part, :weight.shape[0]], weight[...], 1, 0).astype(bf16)


def other_half_kernel(s, own_half, other, weight, out, send_up, send_down):
    rows, half = send_up.shape
    for t in range(NZ // 2):
        tokens = pl.ds(t * 2 * rows, 2 * rows)
        acc = dot(other[tokens, :weight.shape[0]], weight[...], 1, 0) + own_half[tokens, :].astype(f32)
        for c in range(2):
            place = lax.rem(2 * t + c - s[Z] + NZ, NZ)
            out[chunk_rows(place, rows), :] = acc[c * rows:(c + 1) * rows].astype(bf16)
    send_up[...] = out[pl.ds(4 * rows, rows), :half]
    send_down[...] = out[pl.ds(4 * rows, rows), half:]


def first_step_kernel(s, near_up, near_down, below, above, send_up, send_down):
    half = below.shape[1]
    send_up[:, :half] = (near_up[:, :half].astype(f32) + below[...].astype(f32)).astype(bf16)
    send_up[:, half:] = near_up[:, half:]
    send_down[:, :half] = near_down[:, :half]
    send_down[:, half:] = (near_down[:, half:].astype(f32) + above[...].astype(f32)).astype(bf16)


def step_kernel(s, near_up, near_down, below, above, send_up, send_down):
    send_up[...] = (near_up[...].astype(f32) + below[...].astype(f32)).astype(bf16)
    send_down[...] = (near_down[...].astype(f32) + above[...].astype(f32)).astype(bf16)


def hidden_kernel(s, near, below, above, hidden, slope):
    preact = near[...].astype(f32) + below[...].astype(f32) + above[...].astype(f32)
    gelu_value, gelu_slope = gelu_pair(preact)
    hidden[...] = gelu_value.astype(bf16)
    slope[...] = gelu_slope


def grad_pre_kernel(s, near, below, above, slope, grad_pre):
    grad_hidden = (near[...].astype(f32) + below[...].astype(f32) + above[...].astype(f32)).astype(bf16)
    grad_pre[...] = (grad_hidden.astype(f32) * slope[...]).astype(bf16)


def reduce_step(scalars, ring, k, after):
    partial, send_up, send_down = ring
    rows, units = send_up.shape[0], partial.shape[1]

    def near(k):
        return pl.BlockSpec((rows, units), lambda i, s: (k, 0))

    sends = call(
        first_step_kernel if k == 3 else step_kernel, scalars,
        (partial, partial, up(send_up), down(send_down)), (near(k), near(NZ - k), None, None),
        [sds((rows, units))] * 2, after=after,
    )
    return (partial, *sends)


def last_terms(ring):
    partial, send_up, send_down = ring
    return partial, up(send_up), down(send_down)


def halves_kernel(s, above, below, send_up, send_down):
    half = send_up.shape[1]
    send_up[...] = above[:, :half]
    send_down[...] = below[:, half:]


def gather_near(own):
    ups, downs = [own], [own]
    for _ in range(3):
        ups.append(up(ups[-1]))
        downs.append(down(downs[-1]))
    return ups, downs


def gather_far(scalars, ups, downs, after=()):
    rows, units = ups[0].shape
    send_up, send_down = call(
        halves_kernel, scalars, (ups[3], downs[3]), (None, None), [sds((rows, units // 2))] * 2, after=after,
    )
    far = [up(send_up), down(send_down)]
    return [ups[0]] + downs[1:] + far + ups[:0:-1], send_up


def load_chunk(chunks, k):
    if k < 4:
        return chunks[k][...]
    if k == 4:
        return jnp.concatenate([chunks[4][...], chunks[5][...]], 1)
    return chunks[k + 1][...]


def forward_kernel(s, *refs):
    chunks, (weight, own, send_near, send_rest, held) = refs[:9], refs[9:]
    rows = chunks[0].shape[0]
    width = own.shape[1]
    for t in range(NZ // 2):
        left = jnp.concatenate([load_chunk(chunks, 2 * t), load_chunk(chunks, 2 * t + 1)], 0)
        acc = dot(left, weight[...], 1, 0).astype(bf16)
        send = send_near if t < 2 else send_rest
        send[pl.ds(2 * (t % 2) * rows, 2 * rows), :] = acc[:, width:]
        own[pl.ds(2 * t * rows, 2 * rows), :] = acc[:, :width]
        for c in range(2):
            held[chunk_rows(lax.rem(2 * t + c + s[Z], NZ), rows), :] = left[c * rows:(c + 1) * rows]


def outputs_kernel(s, held, weight, own, send):
    width = own.shape[1]
    for t in range(4):
        part = pl.ds(t * 256, 256)
        acc = dot(held[part, :], weight[...], 1, 0).astype(bf16)
        send[part, :] = acc[:, width:]
        own[part, :] = acc[:, :width]


def assemble(s, chunks, held):
    rows = chunks[0].shape[0]
    for k in range(NZ):
        held[chunk_rows(lax.rem(k + s[Z], NZ), rows), :] = load_chunk(chunks, k)


def w_out_kernel(s, *refs):
    chunks, (own, other, keep, core_send, yl_send, held) = refs[:9], refs[9:]
    assemble(s, chunks, held)
    quarter = keep.shape[0]
    low = s[YL] == 0
    for n, (side, stay) in enumerate(((own, keep), (other, core_send))):
        left = side[:, pl.ds(2 * quarter, 2 * quarter)].T
        for t in range(3):
            part = pl.ds(t * 256, 256)
            acc = dot(left, held[:, part], 1, 0)
            a, b = acc[:quarter], acc[quarter:]
            stay[:, part] = jnp.where(low, a, b).astype(bf16)
            yl_send[pl.ds(n * quarter, quarter), part] = jnp.where(low, b, a).astype(bf16)


def w_in_kernel(s, held, own, other, keep, send):
    for source, target in ((other, send), (own, keep)):
        left = source[:, pl.ds(0, keep.shape[0])].T
        for t in range(3):
            part = pl.ds(t * 256, 256)
            target[:, part] = dot(left, held[:, part], 1, 0).astype(bf16)


def merge_kernel(s, out_own, out_sent, gin_own, gin_near, gin_rest, both, held, sems):
    tokens, width = out_own.shape
    rows = tokens // NZ
    copies = []
    for k in range(NZ):
        place = chunk_rows(lax.rem(k + s[Z], NZ), rows)
        sent = (gin_near if k < 4 else gin_rest)[pl.ds(k % 4 * rows, rows), :]
        held[place, :width] = (out_own[place, :].astype(f32) + out_sent[place, :].astype(f32)).astype(bf16)
        held[place, width:] = (gin_own[pl.ds(k * rows, rows), :].astype(f32) + sent.astype(f32)).astype(bf16)
        copy = pltpu.make_async_copy(held.at[place], both.at[place], sems.at[k])
        copy.start()
        copies.append(copy)
    for copy in copies:
        copy.wait()


def total_kernel(s, *refs):
    parts, (out, gin) = refs[:-2], refs[-2:]
    rows, width = out.shape
    acc = jnp.zeros((rows, 2 * width), f32)
    for part in parts:
        for p in range(part.shape[0]):
            acc += part[p].astype(f32)
    out[...] = acc[:, :width].astype(bf16)
    gin[...] = acc[:, width:].astype(bf16)


def join_two_kernel(s, own, sent, out):
    units = own.shape[1]
    out[:, chunk_rows(s[CORE], units)] = own[...]
    out[:, chunk_rows(1 - s[CORE], units)] = sent[...]


def join_four_kernel(s, keep, core_sent, yl_sent, both_sent, out):
    quarter, units = keep.shape
    core, yl = s[CORE], s[YL]
    out[:, chunk_rows(2 * yl + core, units)] = keep[...]
    out[:, chunk_rows(2 * yl + 1 - core, units)] = core_sent[...]
    out[:, chunk_rows(2 * (1 - yl) + core, units)] = yl_sent[pl.ds(0, quarter), :]
    out[:, chunk_rows(2 * (1 - yl) + 1 - core, units)] = both_sent[...]


def on_device(inputs, cotangent, w_in, w_out):
    z, core, yl = lax.axis_index("z"), lax.axis_index("core"), lax.axis_index("yl")
    scalars = jnp.stack([z, core, yl, 2 * yl + core, 2 * yl + 1 - core]).astype(jnp.int32)
    rows, width = inputs.shape
    w_in, w_out = in_hbm(w_in), in_hbm(w_out)
    units = w_in.shape[1] // 4
    tokens = rows * NP
    chunk = tokens // NZ
    half = units // 2

    def w_in_block(which):
        return pl.BlockSpec((width, units), lambda i, s: (0, s[which]))

    def w_out_block(which):
        return pl.BlockSpec((units, width), lambda i, s: (s[which], 0))

    spread, = call(
        spread_kernel, scalars, (in_hbm(inputs), in_hbm(cotangent)), (None, None), [sds((tokens, 2 * width))],
    )
    w_in_send, w_out_send = call(
        copy_kernel, scalars, (w_in, w_out), (w_in_block(THEIRS), w_out_block(THEIRS)),
        [sds((width, units)), sds((units, width))], after=(spread,),
    )
    own = plane_swap(spread)
    other = swap_core(own)
    w_in_other = swap_core(w_in_send)

    work = 4 * tokens * width * units
    partial_outs = [sds((tokens, units)), sds((chunk, half)), sds((chunk, half))]
    piece = sds((chunk, units))
    near = pl.BlockSpec((chunk, units), lambda i, s: (0, 0))
    own_half, = call(
        own_half_kernel, scalars, (own, w_in), (None, w_in_block(MINE)), [sds((tokens, units))], work // 2,
    )
    first = call(
        other_half_kernel, scalars, (own_half, other, w_in_other), (None,) * 3, partial_outs, work // 2,
    )
    square = sds((2 * width, units))
    wi_turned, wo, wo_turned = call(
        arrange_kernel, scalars, (w_in, w_in_other, w_out, swap_core(w_out_send)),
        (w_in_block(MINE), None, w_out_block(MINE), None), [square] * 3, after=(first[1],),
    )
    first = reduce_step(scalars, first, 3, ())
    second = call(
        partial_kernel, scalars, (own, other, wo_turned), (None,) * 3, partial_outs, work, after=(first[1],),
    )
    first = reduce_step(scalars, first, 2, (second[1],))
    second = reduce_step(scalars, second, 3, (first[1],))
    first = reduce_step(scalars, first, 1, (second[1],))
    second = reduce_step(scalars, second, 2, (first[1],))
    hidden_own, slope = call(
        hidden_kernel, scalars, last_terms(first), (near, None, None),
        [piece, sds((chunk, units), f32)], after=(second[1],),
    )
    hidden_near = gather_near(hidden_own)
    hidden, hidden_far = gather_far(scalars, *hidden_near)
    second = reduce_step(scalars, second, 1, (hidden_own,))
    grad_pre_own, = call(
        grad_pre_kernel, scalars, (*last_terms(second), slope), (near, None, None, None), [piece],
        after=(hidden_near[0][1], hidden_near[1][1]),
    )

    half_out = sds((tokens, width))
    quarter = sds((width // 2, units))
    keep, core_send, yl_send, hidden_all = call(
        w_out_kernel, scalars, (*hidden, own, other), (None,) * 11,
        [pltpu.HBM((width // 2, units), bf16), quarter, sds((width, units)), sds((tokens, units))], work,
    )
    yl_sent = lax.ppermute(yl_send, "yl", SWAP)
    core_sent = swap_core(core_send)
    grad_near = gather_near(grad_pre_own)
    grad_pre, far_send = gather_far(scalars, *grad_near, after=(keep,))
    out_own, out_send = call(
        outputs_kernel, scalars, (hidden_all, wo), (None, None), [half_out] * 2, work, after=(grad_pre[4], grad_pre[5]),
    )
    out_sent = swap_core(out_send)

    gin_own, gin_near, gin_rest, grad_pre_all = call(
        forward_kernel, scalars, (*grad_pre, wi_turned), (None,) * 10,
        [half_out, sds((tokens // 2, width)), sds((tokens // 2, width)), pltpu.HBM((tokens, units), bf16)], work, after=(out_send, yl_sent),
    )
    both, = call(
        merge_kernel, scalars, (out_own, out_sent, gin_own, swap_core(gin_near), swap_core(gin_rest)), (None,) * 5,
        [pltpu.HBM((tokens, 2 * width), bf16)], touched=0, after=(yl_sent,),
        out_specs=[pl.BlockSpec(memory_space=pl.ANY)],
        scratch=[pltpu.VMEM((tokens, 2 * width), bf16), pltpu.SemaphoreType.DMA((NZ,))],
    )
    parts = plane_swap(both).reshape(NP, rows, 2 * width)
    gwi_own, gwi_send = call(
        w_in_kernel, scalars, (grad_pre_all, own, other), (None,) * 3,
        [sds((width, units))] * 2, work,
    )
    both_sent = swap_core(yl_sent[width // 2:])
    grad_w_out, = call(
        join_four_kernel, scalars, (keep, core_sent, yl_sent, both_sent), (None,) * 4,
        [sds((width // 2, 4 * units))],
    )
    grad_w_in, = call(
        join_two_kernel, scalars, (gwi_own, swap_core(gwi_send)), (None, None),
        [sds((width, 2 * units))],
    )
    quarters = [
        pl.BlockSpec((NP // 4, rows, 2 * width), functools.partial(lambda q, i, s: (q, 0, 0), q)) for q in range(4)
    ]
    outputs, grad_inputs = call(total_kernel, scalars, (parts,) * 4, quarters, [sds((rows, width))] * 2)
    return outputs, grad_inputs, grad_w_in, grad_w_out.T


def solution(mesh):
    grid = Mesh(mesh.devices.reshape(NZ, 2, 2, 4, 2), ("z", "core", "yh", "x", "yl"))
    row, col = ("z", "core"), ("yh", "x")
    in_specs = (P(PLANE, row), P(PLANE, row), P(row, col), P(col, row))
    out_specs = (P(PLANE, row), P(PLANE, row), P(row, col + ("yl",)), P(col, row + ("yl",)))
    return jax.shard_map(
        on_device, mesh=grid, in_specs=in_specs, out_specs=out_specs, check_vma=False
    )
```

```python
import functools
import math

import jax
import jax.numpy as jnp
from jax import lax
from jax.experimental import pallas as pl
from jax.experimental.pallas import tpu as pltpu
from jax.sharding import Mesh
from jax.sharding import PartitionSpec as P

gelu_c = 0.7978845608028654
gelu_k = 0.044715

NZ = 8
NP = 16
PLANE = ("yl", "yh", "x")
f32 = jnp.float32
bf16 = jnp.bfloat16

UP = [(2 * i + c, 2 * ((i + 1 - 2 * c) % NZ) + c) for i in range(NZ) for c in range(2)]
DOWN = [(b, a) for a, b in UP]
SWAP = [(0, 1), (1, 0)]

Z, CORE, YL, MINE, THEIRS = range(5)


def gelu_pair(preact):
    inner = gelu_c * (preact + gelu_k * preact * preact * preact)
    tangent = jnp.tanh(inner)
    gelu_value = 0.5 * preact * (1.0 + tangent)
    gelu_slope = 0.5 * (1.0 + tangent) + 0.5 * preact * (1.0 - tangent * tangent) * gelu_c * (
        1.0 + 3.0 * gelu_k * preact * preact
    )
    return (gelu_value, gelu_slope)


def up(v):
    return lax.ppermute(v, ("z", "core"), UP)


def down(v):
    return lax.ppermute(v, ("z", "core"), DOWN)


def swap_core(v):
    return lax.ppermute(v, "core", SWAP)


def plane_swap(v):
    return lax.all_to_all(v, PLANE, 0, 0, tiled=True)


def dot(a, b, ca, cb):
    return lax.dot_general(a, b, (((ca,), (cb,)), ((), ())), preferred_element_type=f32)


def in_hbm(v):
    return pltpu.with_memory_space_constraint(v, pltpu.HBM)


def whole(shape):
    return pl.BlockSpec(shape, lambda i, s: (0,) * len(shape), pipeline_mode=pl.Buffered(1))


def whole_out(shape):
    return pl.BlockSpec(shape, lambda i, s: (0, 0))


def call(body, scalars, args, specs, outs, flops=0, after=(), out_specs=None, steps=1, touched=None, scratch=()):
    in_specs = [whole(a.shape) if s is None else s for a, s in zip(args, specs)]
    in_specs += [pl.BlockSpec(memory_space=pl.ANY)] * len(after)
    n = len(args)

    def run(s, *refs):
        body(s, *refs[:n], *refs[n + len(after):])

    if touched is None:
        touched = sum(a.size * a.dtype.itemsize for a in args) + sum(2 * math.prod(o.shape) for o in outs)
    return pl.pallas_call(
        run,
        out_shape=outs,
        grid_spec=pltpu.PrefetchScalarGridSpec(
            num_scalar_prefetch=1,
            grid=(steps,),
            in_specs=in_specs,
            scratch_shapes=scratch,
            out_specs=out_specs or [whole_out(o.shape) for o in outs],
        ),
        compiler_params=pltpu.CompilerParams(vmem_limit_bytes=16 * 1024 * 1024),
        cost_estimate=pl.CostEstimate(flops=flops, bytes_accessed=touched, transcendentals=0),
    )(scalars, *args, *after)


def sds(shape, dtype=bf16):
    return jax.ShapeDtypeStruct(shape, dtype)


def spread_kernel(s, x, dy, spread):
    rows = x.shape[0]
    both = jnp.concatenate([x[...], dy[...]], 1)
    for p in range(NP):
        spread[pl.ds(p * rows, rows), :] = both


def copy_kernel(s, w_in, w_out, w_in_send, w_out_send):
    w_in_send[...] = w_in[...]
    w_out_send[...] = w_out[...]


def arrange_kernel(s, w_in, w_in_other, w_out, w_out_other, wi_turned, wo, wo_turned):
    width = w_in.shape[0]
    for side, (i, o) in enumerate(((w_in, w_out), (w_in_other, w_out_other))):
        part = pl.ds(side * width, width)
        wi_turned[:, part] = i[...].T
        wo[:, part] = o[...]
        wo_turned[part, :] = o[...].T


def distance_of(s, token_chunk):
    steps = token_chunk - s[Z]
    return lax.rem(jnp.where(s[CORE] == 0, steps, -steps) + NZ, NZ)


def chunk_at(s, distance):
    return lax.rem(s[Z] + jnp.where(s[CORE] == 0, distance, NZ - distance), NZ)


def chunk_rows(index, rows):
    return pl.ds(pl.multiple_of(index * rows, rows), rows)


def partial_kernel(s, own, other, weight, out, send_up, send_down):
    rows, half = send_up.shape
    width = weight.shape[0] // 2
    for t in range(NZ // 2):
        tokens = pl.ds(t * 2 * rows, 2 * rows)
        left = jnp.concatenate([own[tokens, width:], other[tokens, width:]], 1)
        acc = dot(left, weight[...], 1, 0).astype(bf16)
        for c in range(2):
            place = distance_of(s, 2 * t + c)
            out[chunk_rows(place, rows), :] = acc[c * rows:(c + 1) * rows]
    send_up[...] = out[pl.ds(4 * rows, rows), :half]
    send_down[...] = out[pl.ds(4 * rows, rows), half:]


def own_half_kernel(s, own, weight, out):
    for t in range(4):
        part = pl.ds(t * 256, 256)
        out[part, :] = dot(own[part, :weight.shape[0]], weight[...], 1, 0).astype(bf16)


def other_half_kernel(s, own_half, other, weight, out, send_up, send_down):
    rows, half = send_up.shape
    for t in range(NZ // 2):
        tokens = pl.ds(t * 2 * rows, 2 * rows)
        acc = dot(other[tokens, :weight.shape[0]], weight[...], 1, 0) + own_half[tokens, :].astype(f32)
        for c in range(2):
            place = distance_of(s, 2 * t + c)
            out[chunk_rows(place, rows), :] = acc[c * rows:(c + 1) * rows].astype(bf16)
    send_up[...] = out[pl.ds(4 * rows, rows), :half]
    send_down[...] = out[pl.ds(4 * rows, rows), half:]


def rows_of(partial, k, rows):
    return partial[pl.ds(k * rows, rows), :]


def first_step_kernel(k, s, partial, below, above, send_up, send_down):
    rows, half = below.shape
    near_up, near_down = rows_of(partial, k, rows), rows_of(partial, NZ - k, rows)
    send_up[:, :half] = (near_up[:, :half].astype(f32) + below[...].astype(f32)).astype(bf16)
    send_up[:, half:] = near_up[:, half:]
    send_down[:, :half] = near_down[:, :half]
    send_down[:, half:] = (near_down[:, half:].astype(f32) + above[...].astype(f32)).astype(bf16)


def step_kernel(k, s, partial, below, above, send_up, send_down):
    rows = below.shape[0]
    send_up[...] = (rows_of(partial, k, rows).astype(f32) + below[...].astype(f32)).astype(bf16)
    send_down[...] = (rows_of(partial, NZ - k, rows).astype(f32) + above[...].astype(f32)).astype(bf16)


def hidden_kernel(s, partial, below, above, hidden, slope):
    rows = below.shape[0]
    preact = rows_of(partial, 0, rows).astype(f32) + below[...].astype(f32) + above[...].astype(f32)
    gelu_value, gelu_slope = gelu_pair(preact)
    hidden[...] = gelu_value.astype(bf16)
    slope[...] = gelu_slope


def grad_pre_kernel(s, partial, below, above, slope, grad_pre):
    rows = below.shape[0]
    total = rows_of(partial, 0, rows).astype(f32) + below[...].astype(f32) + above[...].astype(f32)
    grad_pre[...] = (total.astype(bf16).astype(f32) * slope[...]).astype(bf16)


def reduce_step(scalars, ring, k, after):
    partial, send_up, send_down = ring
    rows, units = send_up.shape[0], partial.shape[1]

    sends = call(
        functools.partial(first_step_kernel if k == 3 else step_kernel, k), scalars,
        (partial, up(send_up), down(send_down)), (None,) * 3, [sds((rows, units))] * 2, after=after,
    )
    return (partial, *sends)


def last_terms(ring):
    partial, send_up, send_down = ring
    return partial, up(send_up), down(send_down)


def halves_kernel(s, above, below, send_up, send_down):
    half = send_up.shape[1]
    send_up[...] = above[:, :half]
    send_down[...] = below[:, half:]


def gather_near(own):
    ups, downs = [own], [own]
    for _ in range(3):
        ups.append(up(ups[-1]))
        downs.append(down(downs[-1]))
    return ups, downs


def gather_far(scalars, ups, downs, after=()):
    rows, units = ups[0].shape
    send_up, send_down = call(
        halves_kernel, scalars, (ups[3], downs[3]), (None, None), [sds((rows, units // 2))] * 2, after=after,
    )
    far = [up(send_up), down(send_down)]
    return [ups[0]] + downs[1:] + far + ups[:0:-1], send_up


def load_chunk(chunks, k):
    if k < 4:
        return chunks[k][...]
    if k == 4:
        return jnp.concatenate([chunks[4][...], chunks[5][...]], 1)
    return chunks[k + 1][...]


def forward_kernel(s, *refs):
    chunks, (weight, own, send_near, send_rest, held, tokens, sems) = refs[:9], refs[9:]
    rows = chunks[0].shape[0]
    width = own.shape[1]
    copies = []
    for t in range(NZ // 2):
        left = jnp.concatenate([load_chunk(chunks, 2 * t), load_chunk(chunks, 2 * t + 1)], 0)
        for c in range(2):
            part = pl.ds((2 * t + c) * rows, rows)
            tokens[part, :] = left[c * rows:(c + 1) * rows]
            place = chunk_rows(chunk_at(s, 2 * t + c), rows)
            copy = pltpu.make_async_copy(tokens.at[part], held.at[place], sems.at[2 * t + c])
            copy.start()
            copies.append(copy)
        acc = dot(left, weight[...], 1, 0).astype(bf16)
        send = send_near if t < 2 else send_rest
        send[pl.ds(2 * (t % 2) * rows, 2 * rows), :] = acc[:, width:]
        own[pl.ds(2 * t * rows, 2 * rows), :] = acc[:, :width]
    for copy in copies:
        copy.wait()


def outputs_kernel(s, held, weight, own, send_near, send_rest):
    width = own.shape[1]
    rows = held.shape[0] // NZ
    for t in range(NZ // 2):
        left = jnp.concatenate(
            [held[chunk_rows(chunk_at(s, 2 * t + c), rows), :] for c in range(2)], 0
        )
        acc = dot(left, weight[...], 1, 0).astype(bf16)
        send = send_near if t < 2 else send_rest
        send[pl.ds(2 * (t % 2) * rows, 2 * rows), :] = acc[:, width:]
        own[pl.ds(2 * t * rows, 2 * rows), :] = acc[:, :width]


def assemble(s, chunks, held):
    rows = chunks[0].shape[0]
    for k in range(NZ):
        held[chunk_rows(chunk_at(s, k), rows), :] = load_chunk(chunks, k)


def w_out_kernel(s, *refs):
    chunks, (own, other, keep, core_send, yl_send, held) = refs[:9], refs[9:]
    assemble(s, chunks, held)
    quarter = keep.shape[0]
    low = s[YL] == 0
    for n, (side, stay) in enumerate(((own, keep), (other, core_send))):
        left = side[:, pl.ds(2 * quarter, 2 * quarter)].T
        for t in range(3):
            part = pl.ds(t * 256, 256)
            acc = dot(left, held[:, part], 1, 0)
            a, b = acc[:quarter], acc[quarter:]
            stay[:, part] = jnp.where(low, a, b).astype(bf16)
            yl_send[pl.ds(n * quarter, quarter), part] = jnp.where(low, b, a).astype(bf16)


def w_in_kernel(s, held, own, other, keep, send):
    for source, target in ((other, send), (own, keep)):
        left = source[:, pl.ds(0, keep.shape[0])].T
        for t in range(3):
            part = pl.ds(t * 256, 256)
            target[:, part] = dot(left, held[:, part], 1, 0).astype(bf16)


def merge_kernel(s, out_own, out_near, out_rest, gin_own, gin_near, gin_rest, both, held, sems):
    tokens, width = out_own.shape
    rows = tokens // NZ
    copies = []
    for k in range(NZ):
        back = (NZ - k) % NZ
        mine, theirs = pl.ds(k * rows, rows), pl.ds(back % 4 * rows, rows)
        for column, own, sent in (
            (0, out_own, out_near if back < 4 else out_rest),
            (width, gin_own, gin_near if back < 4 else gin_rest),
        ):
            total = own[mine, :].astype(f32) + sent[theirs, :].astype(f32)
            held[mine, pl.ds(column, width)] = total.astype(bf16)
        place = chunk_rows(chunk_at(s, k), rows)
        copy = pltpu.make_async_copy(held.at[mine], both.at[place], sems.at[k])
        copy.start()
        copies.append(copy)
    for copy in copies:
        copy.wait()


def total_kernel(s, *refs):
    parts, (out, gin) = refs[:-2], refs[-2:]
    rows, width = out.shape
    acc = jnp.zeros((rows, 2 * width), f32)
    for part in parts:
        for p in range(part.shape[0]):
            acc += part[p].astype(f32)
    out[...] = acc[:, :width].astype(bf16)
    gin[...] = acc[:, width:].astype(bf16)


def join_two_kernel(s, own, sent, out):
    units = own.shape[1]
    out[:, chunk_rows(s[CORE], units)] = own[...]
    out[:, chunk_rows(1 - s[CORE], units)] = sent[...]


def join_four_kernel(s, keep, core_sent, yl_sent, both_sent, out):
    quarter, units = keep.shape
    core, yl = s[CORE], s[YL]
    out[:, chunk_rows(2 * yl + core, units)] = keep[...]
    out[:, chunk_rows(2 * yl + 1 - core, units)] = core_sent[...]
    out[:, chunk_rows(2 * (1 - yl) + core, units)] = yl_sent[pl.ds(0, quarter), :]
    out[:, chunk_rows(2 * (1 - yl) + 1 - core, units)] = both_sent[...]


def on_device(inputs, cotangent, w_in, w_out):
    z, core, yl = lax.axis_index("z"), lax.axis_index("core"), lax.axis_index("yl")
    scalars = jnp.stack([z, core, yl, 2 * yl + core, 2 * yl + 1 - core]).astype(jnp.int32)
    rows, width = inputs.shape
    w_in, w_out = in_hbm(w_in), in_hbm(w_out)
    units = w_in.shape[1] // 4
    tokens = rows * NP
    chunk = tokens // NZ
    half = units // 2

    def w_in_block(which):
        return pl.BlockSpec((width, units), lambda i, s: (0, s[which]))

    def w_out_block(which):
        return pl.BlockSpec((units, width), lambda i, s: (s[which], 0))

    spread, = call(
        spread_kernel, scalars, (in_hbm(inputs), in_hbm(cotangent)), (None, None), [sds((tokens, 2 * width))],
    )
    w_in_send, w_out_send = call(
        copy_kernel, scalars, (w_in, w_out), (w_in_block(THEIRS), w_out_block(THEIRS)),
        [sds((width, units)), sds((units, width))], after=(spread,),
    )
    own = plane_swap(spread)
    other = swap_core(own)
    w_in_other = swap_core(w_in_send)

    work = 4 * tokens * width * units
    partial_outs = [sds((tokens, units)), sds((chunk, half)), sds((chunk, half))]
    piece = sds((chunk, units))
    own_half, = call(
        own_half_kernel, scalars, (own, w_in), (None, w_in_block(MINE)), [sds((tokens, units))], work // 2,
    )
    first = call(
        other_half_kernel, scalars, (own_half, other, w_in_other), (None,) * 3, partial_outs, work // 2,
    )
    square = sds((2 * width, units))
    wi_turned, wo, wo_turned = call(
        arrange_kernel, scalars, (w_in, w_in_other, w_out, swap_core(w_out_send)),
        (w_in_block(MINE), None, w_out_block(MINE), None), [square] * 3, after=(first[1],),
    )
    second = call(
        partial_kernel, scalars, (own, other, wo_turned), (None,) * 3, partial_outs, work, after=(first[1],),
    )
    first = reduce_step(scalars, first, 3, (second[1],))
    second = reduce_step(scalars, second, 3, (first[1],))
    first = reduce_step(scalars, first, 2, (second[1],))
    second = reduce_step(scalars, second, 2, (first[1],))
    first = reduce_step(scalars, first, 1, (second[1],))
    second = reduce_step(scalars, second, 1, (first[1],))
    hidden_own, slope = call(
        hidden_kernel, scalars, last_terms(first), (None,) * 3,
        [piece, sds((chunk, units), f32)],
    )
    hidden_near = gather_near(hidden_own)
    hidden, hidden_far = gather_far(scalars, *hidden_near)
    grad_pre_own, = call(
        grad_pre_kernel, scalars, (*last_terms(second), slope), (None,) * 4, [piece],
        after=(hidden_own,),
    )

    grad_near = gather_near(grad_pre_own)
    grad_pre, far_send = gather_far(scalars, *grad_near)
    half_out, rest_out = sds((tokens, width)), sds((tokens // 2, width))
    quarter = pltpu.HBM((width // 2, units), bf16)
    keep, core_send, yl_send, hidden_all = call(
        w_out_kernel, scalars, (*hidden, own, other), (None,) * 11,
        [quarter, quarter, sds((width, units)), sds((tokens, units))], work,
        after=(far_send,),
    )
    yl_sent = lax.ppermute(yl_send, "yl", SWAP)
    core_sent = swap_core(core_send)
    out_own, *out_send = call(
        outputs_kernel, scalars, (hidden_all, wo), (None, None), [half_out, rest_out, rest_out], touched=0, after=(yl_send, grad_pre[4], grad_pre[5]),
    )
    out_sent = [swap_core(half) for half in out_send]

    gin_own, gin_near, gin_rest, grad_pre_all = call(
        forward_kernel, scalars, (*grad_pre, wi_turned), (None,) * 10,
        [half_out, rest_out, rest_out, pltpu.HBM((tokens, units), bf16)], touched=0, after=(out_send[0],),
        out_specs=[whole_out((tokens, width))] + [whole_out((tokens // 2, width))] * 2
        + [pl.BlockSpec(memory_space=pl.ANY)],
        scratch=[pltpu.VMEM((tokens, units), bf16), pltpu.SemaphoreType.DMA((NZ,))],
    )
    both, = call(
        merge_kernel, scalars, (out_own, *out_sent, gin_own, swap_core(gin_near), swap_core(gin_rest)), (None,) * 6,
        [pltpu.HBM((tokens, 2 * width), bf16)], touched=0, after=(yl_sent,),
        out_specs=[pl.BlockSpec(memory_space=pl.ANY)],
        scratch=[pltpu.VMEM((tokens, 2 * width), bf16), pltpu.SemaphoreType.DMA((NZ,))],
    )
    parts = plane_swap(both).reshape(NP, rows, 2 * width)
    gwi_own, gwi_send = call(
        w_in_kernel, scalars, (grad_pre_all, own, other), (None,) * 3,
        [sds((width, units))] * 2, work,
    )
    both_sent = swap_core(yl_sent[width // 2:])
    grad_w_out, = call(
        join_four_kernel, scalars, (keep, core_sent, yl_sent, both_sent), (None,) * 4,
        [sds((width // 2, 4 * units))],
    )
    grad_w_in, = call(
        join_two_kernel, scalars, (gwi_own, swap_core(gwi_send)), (None, None),
        [sds((width, 2 * units))],
    )
    quarters = [
        pl.BlockSpec((NP // 4, rows, 2 * width), functools.partial(lambda q, i, s: (q, 0, 0), q)) for q in range(4)
    ]
    outputs, grad_inputs = call(total_kernel, scalars, (parts,) * 4, quarters, [sds((rows, width))] * 2)
    return outputs, grad_inputs, grad_w_in, grad_w_out.T


def solution(mesh):
    grid = Mesh(mesh.devices.reshape(NZ, 2, 2, 4, 2), ("z", "core", "yh", "x", "yl"))
    row, col = ("z", "core"), ("yh", "x")
    in_specs = (P(PLANE, row), P(PLANE, row), P(row, col), P(col, row))
    out_specs = (P(PLANE, row), P(PLANE, row), P(row, col + ("yl",)), P(col, row + ("yl",)))
    return jax.shard_map(
        on_device, mesh=grid, in_specs=in_specs, out_specs=out_specs, check_vma=False
    )
```

```python
import functools
import math

import jax
import jax.numpy as jnp
from jax import lax
from jax.experimental import pallas as pl
from jax.experimental.pallas import tpu as pltpu
from jax.sharding import Mesh
from jax.sharding import PartitionSpec as P

gelu_c = 0.7978845608028654
gelu_k = 0.044715

NZ = 8
NP = 16
PLANE = ("yl", "yh", "x")
f32 = jnp.float32
bf16 = jnp.bfloat16

UP = [(2 * i + c, 2 * ((i + 1 - 2 * c) % NZ) + c) for i in range(NZ) for c in range(2)]
DOWN = [(b, a) for a, b in UP]
SWAP = [(0, 1), (1, 0)]

Z, CORE, YL, MINE, THEIRS = range(5)


def gelu_pair(preact):
    inner = gelu_c * (preact + gelu_k * preact * preact * preact)
    tangent = jnp.tanh(inner)
    gelu_value = 0.5 * preact * (1.0 + tangent)
    gelu_slope = 0.5 * (1.0 + tangent) + 0.5 * preact * (1.0 - tangent * tangent) * gelu_c * (
        1.0 + 3.0 * gelu_k * preact * preact
    )
    return (gelu_value, gelu_slope)


def up(v):
    return lax.ppermute(v, ("z", "core"), UP)


def down(v):
    return lax.ppermute(v, ("z", "core"), DOWN)


def swap_core(v):
    return lax.ppermute(v, "core", SWAP)


def plane_swap(v):
    return lax.all_to_all(v, PLANE, 0, 0, tiled=True)


def dot(a, b, ca, cb):
    return lax.dot_general(a, b, (((ca,), (cb,)), ((), ())), preferred_element_type=f32)


def in_hbm(v):
    return pltpu.with_memory_space_constraint(v, pltpu.HBM)


def whole(shape):
    return pl.BlockSpec(shape, lambda i, s: (0,) * len(shape), pipeline_mode=pl.Buffered(1))


def whole_out(shape):
    return pl.BlockSpec(shape, lambda i, s: (0, 0))


def call(body, scalars, args, specs, outs, flops=0, after=(), out_specs=None, steps=1, touched=None, scratch=()):
    in_specs = [whole(a.shape) if s is None else s for a, s in zip(args, specs)]
    in_specs += [pl.BlockSpec(memory_space=pl.ANY)] * len(after)
    n = len(args)

    def run(s, *refs):
        body(s, *refs[:n], *refs[n + len(after):])

    if touched is None:
        touched = sum(a.size * a.dtype.itemsize for a in args) + sum(2 * math.prod(o.shape) for o in outs)
    return pl.pallas_call(
        run,
        out_shape=outs,
        grid_spec=pltpu.PrefetchScalarGridSpec(
            num_scalar_prefetch=1,
            grid=(steps,),
            in_specs=in_specs,
            scratch_shapes=scratch,
            out_specs=out_specs or [whole_out(o.shape) for o in outs],
        ),
        compiler_params=pltpu.CompilerParams(vmem_limit_bytes=16 * 1024 * 1024),
        cost_estimate=pl.CostEstimate(flops=flops, bytes_accessed=touched, transcendentals=0),
    )(scalars, *args, *after)


def sds(shape, dtype=bf16):
    return jax.ShapeDtypeStruct(shape, dtype)


def spread_kernel(s, x, dy, spread):
    rows = x.shape[0]
    both = jnp.concatenate([x[...], dy[...]], 1)
    for p in range(NP):
        spread[pl.ds(p * rows, rows), :] = both


def copy_kernel(s, w_in, w_out, w_in_send, w_out_send):
    w_in_send[...] = w_in[...]
    w_out_send[...] = w_out[...]


def arrange_kernel(s, w_in, w_in_other, w_out, w_out_other, wi_turned, wo, wo_turned):
    width = w_in.shape[0]
    for side, (i, o) in enumerate(((w_in, w_out), (w_in_other, w_out_other))):
        part = pl.ds(side * width, width)
        wi_turned[:, part] = i[...].T
        wo[:, part] = o[...]
        wo_turned[part, :] = o[...].T


def distance_of(s, token_chunk):
    steps = token_chunk - s[Z]
    return lax.rem(jnp.where(s[CORE] == 0, steps, -steps) + NZ, NZ)


def chunk_at(s, distance):
    return lax.rem(s[Z] + jnp.where(s[CORE] == 0, distance, NZ - distance), NZ)


def chunk_rows(index, rows):
    return pl.ds(pl.multiple_of(index * rows, rows), rows)


def partial_kernel(s, own, other, weight, out, send_up, send_down):
    rows, half = send_up.shape
    width = weight.shape[0] // 2
    for t in range(NZ // 2):
        tokens = pl.ds(t * 2 * rows, 2 * rows)
        left = jnp.concatenate([own[tokens, width:], other[tokens, width:]], 1)
        acc = dot(left, weight[...], 1, 0).astype(bf16)
        for c in range(2):
            place = distance_of(s, 2 * t + c)
            out[chunk_rows(place, rows), :] = acc[c * rows:(c + 1) * rows]
    send_up[...] = out[pl.ds(4 * rows, rows), :half]
    send_down[...] = out[pl.ds(4 * rows, rows), half:]


def own_half_kernel(s, own, weight, out):
    for t in range(4):
        part = pl.ds(t * 256, 256)
        out[part, :] = dot(own[part, :weight.shape[0]], weight[...], 1, 0).astype(bf16)


def other_half_kernel(s, own_half, other, weight, out, send_up, send_down):
    rows, half = send_up.shape
    for t in range(NZ // 2):
        tokens = pl.ds(t * 2 * rows, 2 * rows)
        acc = dot(other[tokens, :weight.shape[0]], weight[...], 1, 0) + own_half[tokens, :].astype(f32)
        for c in range(2):
            place = distance_of(s, 2 * t + c)
            out[chunk_rows(place, rows), :] = acc[c * rows:(c + 1) * rows].astype(bf16)
    send_up[...] = out[pl.ds(4 * rows, rows), :half]
    send_down[...] = out[pl.ds(4 * rows, rows), half:]


def rows_of(partial, k, rows):
    return partial[pl.ds(k * rows, rows), :]


def first_step_kernel(k, s, partial, below, above, send_up, send_down):
    rows, half = below.shape
    near_up, near_down = rows_of(partial, k, rows), rows_of(partial, NZ - k, rows)
    send_up[:, :half] = (near_up[:, :half].astype(f32) + below[...].astype(f32)).astype(bf16)
    send_up[:, half:] = near_up[:, half:]
    send_down[:, :half] = near_down[:, :half]
    send_down[:, half:] = (near_down[:, half:].astype(f32) + above[...].astype(f32)).astype(bf16)


def step_kernel(k, s, partial, below, above, send_up, send_down):
    rows = below.shape[0]
    send_up[...] = (rows_of(partial, k, rows).astype(f32) + below[...].astype(f32)).astype(bf16)
    send_down[...] = (rows_of(partial, NZ - k, rows).astype(f32) + above[...].astype(f32)).astype(bf16)


def hidden_kernel(s, partial, below, above, hidden, slope):
    rows = below.shape[0]
    preact = rows_of(partial, 0, rows).astype(f32) + below[...].astype(f32) + above[...].astype(f32)
    gelu_value, gelu_slope = gelu_pair(preact)
    hidden[...] = gelu_value.astype(bf16)
    slope[...] = gelu_slope


def grad_pre_kernel(s, partial, below, above, slope, grad_pre):
    rows = below.shape[0]
    total = rows_of(partial, 0, rows).astype(f32) + below[...].astype(f32) + above[...].astype(f32)
    grad_pre[...] = (total.astype(bf16).astype(f32) * slope[...]).astype(bf16)


def reduce_step(scalars, ring, k, after):
    partial, send_up, send_down = ring
    rows, units = send_up.shape[0], partial.shape[1]

    sends = call(
        functools.partial(first_step_kernel if k == 3 else step_kernel, k), scalars,
        (partial, up(send_up), down(send_down)), (None,) * 3, [sds((rows, units))] * 2, after=after,
    )
    return (partial, *sends)


def last_terms(ring):
    partial, send_up, send_down = ring
    return partial, up(send_up), down(send_down)


def halves_kernel(s, above, below, send_up, send_down):
    half = send_up.shape[1]
    send_up[...] = above[:, :half]
    send_down[...] = below[:, half:]


def gather_near(own):
    ups, downs = [own], [own]
    for _ in range(3):
        ups.append(up(ups[-1]))
        downs.append(down(downs[-1]))
    return ups, downs


def gather_far(scalars, ups, downs, after=()):
    rows, units = ups[0].shape
    send_up, send_down = call(
        halves_kernel, scalars, (ups[3], downs[3]), (None, None), [sds((rows, units // 2))] * 2, after=after,
    )
    far = [up(send_up), down(send_down)]
    return [ups[0]] + downs[1:] + far + ups[:0:-1], send_up


def load_chunk(chunks, k):
    if k < 4:
        return chunks[k][...]
    if k == 4:
        return jnp.concatenate([chunks[4][...], chunks[5][...]], 1)
    return chunks[k + 1][...]


def forward_kernel(s, *refs):
    chunks, (weight, own, send_near, send_rest, held) = refs[:9], refs[9:]
    rows = chunks[0].shape[0]
    width = own.shape[1]
    for t in range(NZ // 2):
        left = jnp.concatenate([load_chunk(chunks, 2 * t), load_chunk(chunks, 2 * t + 1)], 0)
        acc = dot(left, weight[...], 1, 0).astype(bf16)
        send = send_near if t < 2 else send_rest
        send[pl.ds(2 * (t % 2) * rows, 2 * rows), :] = acc[:, width:]
        own[pl.ds(2 * t * rows, 2 * rows), :] = acc[:, :width]
        for c in range(2):
            held[chunk_rows(chunk_at(s, 2 * t + c), rows), :] = left[c * rows:(c + 1) * rows]


def outputs_kernel(s, held, weight, own, send_near, send_rest):
    width = own.shape[1]
    rows = held.shape[0] // NZ
    for t in range(NZ // 2):
        left = jnp.concatenate(
            [held[chunk_rows(chunk_at(s, 2 * t + c), rows), :] for c in range(2)], 0
        )
        acc = dot(left, weight[...], 1, 0).astype(bf16)
        send = send_near if t < 2 else send_rest
        send[pl.ds(2 * (t % 2) * rows, 2 * rows), :] = acc[:, width:]
        own[pl.ds(2 * t * rows, 2 * rows), :] = acc[:, :width]


def assemble(s, chunks, held):
    rows = chunks[0].shape[0]
    for k in range(NZ):
        held[chunk_rows(chunk_at(s, k), rows), :] = load_chunk(chunks, k)


def w_out_kernel(s, *refs):
    chunks, (own, other, keep, core_send, yl_send, held) = refs[:9], refs[9:]
    assemble(s, chunks, held)
    quarter = keep.shape[0]
    low = s[YL] == 0
    for n, (side, stay) in enumerate(((own, keep), (other, core_send))):
        left = side[:, pl.ds(2 * quarter, 2 * quarter)].T
        for t in range(3):
            part = pl.ds(t * 256, 256)
            acc = dot(left, held[:, part], 1, 0)
            a, b = acc[:quarter], acc[quarter:]
            stay[:, part] = jnp.where(low, a, b).astype(bf16)
            yl_send[pl.ds(n * quarter, quarter), part] = jnp.where(low, b, a).astype(bf16)


def w_in_kernel(s, held, own, other, keep, send):
    for source, target in ((other, send), (own, keep)):
        left = source[:, pl.ds(0, keep.shape[0])].T
        for t in range(3):
            part = pl.ds(t * 256, 256)
            target[:, part] = dot(left, held[:, part], 1, 0).astype(bf16)


def merge_kernel(s, out_own, out_near, out_rest, gin_own, gin_near, gin_rest, both, held, sems):
    tokens, width = out_own.shape
    rows = tokens // NZ
    copies = []
    for k in range(NZ):
        back = (NZ - k) % NZ
        mine, theirs = pl.ds(k * rows, rows), pl.ds(back % 4 * rows, rows)
        for column, own, sent in (
            (0, out_own, out_near if back < 4 else out_rest),
            (width, gin_own, gin_near if back < 4 else gin_rest),
        ):
            total = own[mine, :].astype(f32) + sent[theirs, :].astype(f32)
            held[mine, pl.ds(column, width)] = total.astype(bf16)
        place = chunk_rows(chunk_at(s, k), rows)
        copy = pltpu.make_async_copy(held.at[mine], both.at[place], sems.at[k])
        copy.start()
        copies.append(copy)
    for copy in copies:
        copy.wait()


def total_kernel(s, *refs):
    parts, (out, gin) = refs[:-2], refs[-2:]
    rows, width = out.shape
    acc = jnp.zeros((rows, 2 * width), f32)
    for part in parts:
        for p in range(part.shape[0]):
            acc += part[p].astype(f32)
    out[...] = acc[:, :width].astype(bf16)
    gin[...] = acc[:, width:].astype(bf16)


def join_two_kernel(s, own, sent, out):
    units = own.shape[1]
    out[:, chunk_rows(s[CORE], units)] = own[...]
    out[:, chunk_rows(1 - s[CORE], units)] = sent[...]


def join_four_kernel(s, keep, core_sent, yl_sent, both_sent, out):
    quarter, units = keep.shape
    core, yl = s[CORE], s[YL]
    out[:, chunk_rows(2 * yl + core, units)] = keep[...]
    out[:, chunk_rows(2 * yl + 1 - core, units)] = core_sent[...]
    out[:, chunk_rows(2 * (1 - yl) + core, units)] = yl_sent[pl.ds(0, quarter), :]
    out[:, chunk_rows(2 * (1 - yl) + 1 - core, units)] = both_sent[...]


def on_device(inputs, cotangent, w_in, w_out):
    z, core, yl = lax.axis_index("z"), lax.axis_index("core"), lax.axis_index("yl")
    scalars = jnp.stack([z, core, yl, 2 * yl + core, 2 * yl + 1 - core]).astype(jnp.int32)
    rows, width = inputs.shape
    w_in, w_out = in_hbm(w_in), in_hbm(w_out)
    units = w_in.shape[1] // 4
    tokens = rows * NP
    chunk = tokens // NZ
    half = units // 2

    def w_in_block(which):
        return pl.BlockSpec((width, units), lambda i, s: (0, s[which]))

    def w_out_block(which):
        return pl.BlockSpec((units, width), lambda i, s: (s[which], 0))

    spread, = call(
        spread_kernel, scalars, (in_hbm(inputs), in_hbm(cotangent)), (None, None), [sds((tokens, 2 * width))],
    )
    w_in_send, w_out_send = call(
        copy_kernel, scalars, (w_in, w_out), (w_in_block(THEIRS), w_out_block(THEIRS)),
        [sds((width, units)), sds((units, width))], after=(spread,),
    )
    own = plane_swap(spread)
    other = swap_core(own)
    w_in_other = swap_core(w_in_send)

    work = 4 * tokens * width * units
    partial_outs = [sds((tokens, units)), sds((chunk, half)), sds((chunk, half))]
    piece = sds((chunk, units))
    own_half, = call(
        own_half_kernel, scalars, (own, w_in), (None, w_in_block(MINE)), [sds((tokens, units))], work // 2,
    )
    first = call(
        other_half_kernel, scalars, (own_half, other, w_in_other), (None,) * 3, partial_outs, work // 2,
    )
    square = sds((2 * width, units))
    wi_turned, wo, wo_turned = call(
        arrange_kernel, scalars, (w_in, w_in_other, w_out, swap_core(w_out_send)),
        (w_in_block(MINE), None, w_out_block(MINE), None), [square] * 3, after=(first[1],),
    )
    second = call(
        partial_kernel, scalars, (own, other, wo_turned), (None,) * 3, partial_outs, work, after=(first[1],),
    )
    first = reduce_step(scalars, first, 3, (second[1],))
    second = reduce_step(scalars, second, 3, (first[1],))
    first = reduce_step(scalars, first, 2, (second[1],))
    second = reduce_step(scalars, second, 2, (first[1],))
    first = reduce_step(scalars, first, 1, (second[1],))
    second = reduce_step(scalars, second, 1, (first[1],))
    hidden_own, slope = call(
        hidden_kernel, scalars, last_terms(first), (None,) * 3,
        [piece, sds((chunk, units), f32)],
    )
    hidden_near = gather_near(hidden_own)
    hidden, hidden_far = gather_far(scalars, *hidden_near)
    grad_pre_own, = call(
        grad_pre_kernel, scalars, (*last_terms(second), slope), (None,) * 4, [piece],
        after=(hidden_own,),
    )

    grad_near = gather_near(grad_pre_own)
    grad_pre, far_send = gather_far(scalars, *grad_near)
    half_out, rest_out = sds((tokens, width)), sds((tokens // 2, width))
    quarter = pltpu.HBM((width // 2, units), bf16)
    keep, core_send, yl_send, hidden_all = call(
        w_out_kernel, scalars, (*hidden, own, other), (None,) * 11,
        [quarter, quarter, sds((width, units)), sds((tokens, units))], work,
        after=(far_send,),
    )
    yl_sent = lax.ppermute(yl_send, "yl", SWAP)
    core_sent = swap_core(core_send)
    out_own, *out_send = call(
        outputs_kernel, scalars, (hidden_all, wo), (None, None), [half_out, rest_out, rest_out], work, after=(yl_send, grad_pre[4], grad_pre[5]),
    )
    out_sent = [swap_core(half) for half in out_send]

    gin_own, gin_near, gin_rest, grad_pre_all = call(
        forward_kernel, scalars, (*grad_pre, wi_turned), (None,) * 10,
        [half_out, rest_out, rest_out, sds((tokens, units))], work, after=(out_send[0],),
    )
    both, = call(
        merge_kernel, scalars, (out_own, *out_sent, gin_own, swap_core(gin_near), swap_core(gin_rest)), (None,) * 6,
        [pltpu.HBM((tokens, 2 * width), bf16)], touched=0, after=(yl_sent,),
        out_specs=[pl.BlockSpec(memory_space=pl.ANY)],
        scratch=[pltpu.VMEM((tokens, 2 * width), bf16), pltpu.SemaphoreType.DMA((NZ,))],
    )
    parts = plane_swap(both).reshape(NP, rows, 2 * width)
    gwi_own, gwi_send = call(
        w_in_kernel, scalars, (grad_pre_all, own, other), (None,) * 3,
        [sds((width, units))] * 2, work,
    )
    both_sent = swap_core(yl_sent[width // 2:])
    grad_w_out, = call(
        join_four_kernel, scalars, (keep, core_sent, yl_sent, both_sent), (None,) * 4,
        [sds((width // 2, 4 * units))],
    )
    grad_w_in, = call(
        join_two_kernel, scalars, (gwi_own, swap_core(gwi_send)), (None, None),
        [sds((width, 2 * units))],
    )
    quarters = [
        pl.BlockSpec((NP // 4, rows, 2 * width), functools.partial(lambda q, i, s: (q, 0, 0), q)) for q in range(4)
    ]
    outputs, grad_inputs = call(total_kernel, scalars, (parts,) * 4, quarters, [sds((rows, width))] * 2)
    return outputs, grad_inputs, grad_w_in, grad_w_out.T


def solution(mesh):
    grid = Mesh(mesh.devices.reshape(NZ, 2, 2, 4, 2), ("z", "core", "yh", "x", "yl"))
    row, col = ("z", "core"), ("yh", "x")
    in_specs = (P(PLANE, row), P(PLANE, row), P(row, col), P(col, row))
    out_specs = (P(PLANE, row), P(PLANE, row), P(row, col + ("yl",)), P(col, row + ("yl",)))
    return jax.shard_map(
        on_device, mesh=grid, in_specs=in_specs, out_specs=out_specs, check_vma=False
    )
```

```python
import functools
import math

import jax
import jax.numpy as jnp
from jax import lax
from jax.experimental import pallas as pl
from jax.experimental.pallas import tpu as pltpu
from jax.sharding import Mesh
from jax.sharding import PartitionSpec as P

gelu_c = 0.7978845608028654
gelu_k = 0.044715

NZ = 8
NP = 16
PLANE = ("yl", "yh", "x")
f32 = jnp.float32
bf16 = jnp.bfloat16

UP = [(2 * i + c, 2 * ((i + 1 - 2 * c) % NZ) + c) for i in range(NZ) for c in range(2)]
DOWN = [(b, a) for a, b in UP]
SWAP = [(0, 1), (1, 0)]

Z, CORE, YL, MINE, THEIRS = range(5)


def gelu_pair(preact):
    inner = gelu_c * (preact + gelu_k * preact * preact * preact)
    tangent = jnp.tanh(inner)
    gelu_value = 0.5 * preact * (1.0 + tangent)
    gelu_slope = 0.5 * (1.0 + tangent) + 0.5 * preact * (1.0 - tangent * tangent) * gelu_c * (
        1.0 + 3.0 * gelu_k * preact * preact
    )
    return (gelu_value, gelu_slope)


def up(v):
    return lax.ppermute(v, ("z", "core"), UP)


def down(v):
    return lax.ppermute(v, ("z", "core"), DOWN)


def swap_core(v):
    return lax.ppermute(v, "core", SWAP)


def plane_swap(v):
    return lax.all_to_all(v, PLANE, 0, 0, tiled=True)


def dot(a, b, ca, cb):
    return lax.dot_general(a, b, (((ca,), (cb,)), ((), ())), preferred_element_type=f32)


def in_hbm(v):
    return pltpu.with_memory_space_constraint(v, pltpu.HBM)


def whole(shape):
    return pl.BlockSpec(shape, lambda i, s: (0,) * len(shape), pipeline_mode=pl.Buffered(1))


def whole_out(shape):
    return pl.BlockSpec(shape, lambda i, s: (0, 0))


def call(body, scalars, args, specs, outs, flops=0, after=(), out_specs=None, steps=1, touched=None, scratch=()):
    in_specs = [whole(a.shape) if s is None else s for a, s in zip(args, specs)]
    in_specs += [pl.BlockSpec(memory_space=pl.ANY)] * len(after)
    n = len(args)

    def run(s, *refs):
        body(s, *refs[:n], *refs[n + len(after):])

    if touched is None:
        touched = sum(a.size * a.dtype.itemsize for a in args) + sum(2 * math.prod(o.shape) for o in outs)
    return pl.pallas_call(
        run,
        out_shape=outs,
        grid_spec=pltpu.PrefetchScalarGridSpec(
            num_scalar_prefetch=1,
            grid=(steps,),
            in_specs=in_specs,
            scratch_shapes=scratch,
            out_specs=out_specs or [whole_out(o.shape) for o in outs],
        ),
        compiler_params=pltpu.CompilerParams(vmem_limit_bytes=16 * 1024 * 1024),
        cost_estimate=pl.CostEstimate(flops=flops, bytes_accessed=touched, transcendentals=0),
    )(scalars, *args, *after)


def sds(shape, dtype=bf16):
    return jax.ShapeDtypeStruct(shape, dtype)


def prepare_kernel(s, w_in, w_out, x, dy, w_in_send, w_out_send, spread):
    w_in_send[...] = w_in[...]
    w_out_send[...] = w_out[...]
    rows = x.shape[0]
    both = jnp.concatenate([x[...], dy[...]], 1)
    for p in range(NP):
        spread[pl.ds(p * rows, rows), :] = both


def arrange_kernel(s, w_in, w_in_other, w_out, w_out_other, wi_turned, wo, wo_turned):
    width = w_in.shape[0]
    for side, (i, o) in enumerate(((w_in, w_out), (w_in_other, w_out_other))):
        part = pl.ds(side * width, width)
        wi_turned[:, part] = i[...].T
        wo[:, part] = o[...]
        wo_turned[part, :] = o[...].T


def distance_of(s, token_chunk):
    steps = token_chunk - s[Z]
    return lax.rem(jnp.where(s[CORE] == 0, steps, -steps) + NZ, NZ)


def chunk_at(s, distance):
    return lax.rem(s[Z] + jnp.where(s[CORE] == 0, distance, NZ - distance), NZ)


def chunk_rows(index, rows):
    return pl.ds(pl.multiple_of(index * rows, rows), rows)


def partial_kernel(s, own, other, weight, out, send_up, send_down):
    rows, half = send_up.shape
    width = weight.shape[0] // 2
    for t in range(NZ // 2):
        tokens = pl.ds(t * 2 * rows, 2 * rows)
        left = jnp.concatenate([own[tokens, width:], other[tokens, width:]], 1)
        acc = dot(left, weight[...], 1, 0).astype(bf16)
        for c in range(2):
            place = distance_of(s, 2 * t + c)
            out[chunk_rows(place, rows), :] = acc[c * rows:(c + 1) * rows]
    send_up[...] = out[pl.ds(4 * rows, rows), :half]
    send_down[...] = out[pl.ds(4 * rows, rows), half:]


def own_half_kernel(s, own, weight, out):
    for t in range(4):
        part = pl.ds(t * 256, 256)
        out[part, :] = dot(own[part, :weight.shape[0]], weight[...], 1, 0).astype(bf16)


def other_half_kernel(s, own_half, other, weight, out, send_up, send_down):
    rows, half = send_up.shape
    for t in range(NZ // 2):
        tokens = pl.ds(t * 2 * rows, 2 * rows)
        acc = dot(other[tokens, :weight.shape[0]], weight[...], 1, 0) + own_half[tokens, :].astype(f32)
        for c in range(2):
            place = distance_of(s, 2 * t + c)
            out[chunk_rows(place, rows), :] = acc[c * rows:(c + 1) * rows].astype(bf16)
    send_up[...] = out[pl.ds(4 * rows, rows), :half]
    send_down[...] = out[pl.ds(4 * rows, rows), half:]


def rows_of(partial, k, rows):
    return partial[pl.ds(k * rows, rows), :]


def first_step_kernel(k, s, partial, below, above, send_up, send_down):
    rows, half = below.shape
    near_up, near_down = rows_of(partial, k, rows), rows_of(partial, NZ - k, rows)
    send_up[:, :half] = (near_up[:, :half].astype(f32) + below[...].astype(f32)).astype(bf16)
    send_up[:, half:] = near_up[:, half:]
    send_down[:, :half] = near_down[:, :half]
    send_down[:, half:] = (near_down[:, half:].astype(f32) + above[...].astype(f32)).astype(bf16)


def step_kernel(k, s, partial, below, above, send_up, send_down):
    rows = below.shape[0]
    send_up[...] = (rows_of(partial, k, rows).astype(f32) + below[...].astype(f32)).astype(bf16)
    send_down[...] = (rows_of(partial, NZ - k, rows).astype(f32) + above[...].astype(f32)).astype(bf16)


def hidden_kernel(s, partial, below, above, hidden, slope):
    rows = below.shape[0]
    preact = rows_of(partial, 0, rows).astype(f32) + below[...].astype(f32) + above[...].astype(f32)
    gelu_value, gelu_slope = gelu_pair(preact)
    hidden[...] = gelu_value.astype(bf16)
    slope[...] = gelu_slope


def grad_pre_kernel(s, partial, below, above, slope, grad_pre):
    rows = below.shape[0]
    total = rows_of(partial, 0, rows).astype(f32) + below[...].astype(f32) + above[...].astype(f32)
    grad_pre[...] = (total.astype(bf16).astype(f32) * slope[...]).astype(bf16)


def reduce_step(scalars, ring, k, after):
    partial, send_up, send_down = ring
    rows, units = send_up.shape[0], partial.shape[1]

    sends = call(
        functools.partial(first_step_kernel if k == 3 else step_kernel, k), scalars,
        (partial, up(send_up), down(send_down)), (None,) * 3, [sds((rows, units))] * 2, after=after,
    )
    return (partial, *sends)


def last_terms(ring):
    partial, send_up, send_down = ring
    return partial, up(send_up), down(send_down)


def halves_kernel(s, above, below, send_up, send_down):
    half = send_up.shape[1]
    send_up[...] = above[:, :half]
    send_down[...] = below[:, half:]


def gather_near(own):
    ups, downs = [own], [own]
    for _ in range(3):
        ups.append(up(ups[-1]))
        downs.append(down(downs[-1]))
    return ups, downs


def gather_far(scalars, ups, downs, after=()):
    rows, units = ups[0].shape
    send_up, send_down = call(
        halves_kernel, scalars, (ups[3], downs[3]), (None, None), [sds((rows, units // 2))] * 2, after=after,
    )
    far = [up(send_up), down(send_down)]
    return [ups[0]] + downs[1:] + far + ups[:0:-1], send_up


def load_chunk(chunks, k):
    if k < 4:
        return chunks[k][...]
    if k == 4:
        return jnp.concatenate([chunks[4][...], chunks[5][...]], 1)
    return chunks[k + 1][...]


def forward_kernel(s, *refs):
    chunks, (weight, own, send_near, send_rest, held) = refs[:9], refs[9:]
    rows = chunks[0].shape[0]
    width = own.shape[1]
    for t in range(NZ // 2):
        left = jnp.concatenate([load_chunk(chunks, 2 * t), load_chunk(chunks, 2 * t + 1)], 0)
        acc = dot(left, weight[...], 1, 0).astype(bf16)
        send = send_near if t < 2 else send_rest
        send[pl.ds(2 * (t % 2) * rows, 2 * rows), :] = acc[:, width:]
        own[pl.ds(2 * t * rows, 2 * rows), :] = acc[:, :width]
        for c in range(2):
            held[chunk_rows(chunk_at(s, 2 * t + c), rows), :] = left[c * rows:(c + 1) * rows]


def outputs_kernel(s, held, weight, own, send_near, send_rest):
    width = own.shape[1]
    rows = held.shape[0] // NZ
    for t in range(NZ // 2):
        left = jnp.concatenate(
            [held[chunk_rows(chunk_at(s, 2 * t + c), rows), :] for c in range(2)], 0
        )
        acc = dot(left, weight[...], 1, 0).astype(bf16)
        send = send_near if t < 2 else send_rest
        send[pl.ds(2 * (t % 2) * rows, 2 * rows), :] = acc[:, width:]
        own[pl.ds(2 * t * rows, 2 * rows), :] = acc[:, :width]


def assemble(s, chunks, held):
    rows = chunks[0].shape[0]
    for k in range(NZ):
        held[chunk_rows(chunk_at(s, k), rows), :] = load_chunk(chunks, k)


def w_out_kernel(s, *refs):
    chunks, (own, other, keep, core_send, yl_send, held) = refs[:9], refs[9:]
    assemble(s, chunks, held)
    quarter = keep.shape[0]
    low = s[YL] == 0
    for n, (side, stay) in enumerate(((own, keep), (other, core_send))):
        left = side[:, pl.ds(2 * quarter, 2 * quarter)].T
        for t in range(3):
            part = pl.ds(t * 256, 256)
            acc = dot(left, held[:, part], 1, 0)
            a, b = acc[:quarter], acc[quarter:]
            stay[:, part] = jnp.where(low, a, b).astype(bf16)
            yl_send[pl.ds(n * quarter, quarter), part] = jnp.where(low, b, a).astype(bf16)


def w_in_kernel(s, held, own, other, keep, send):
    for source, target in ((other, send), (own, keep)):
        left = source[:, pl.ds(0, keep.shape[0])].T
        for t in range(3):
            part = pl.ds(t * 256, 256)
            target[:, part] = dot(left, held[:, part], 1, 0).astype(bf16)


def merge_kernel(s, out_own, out_near, out_rest, gin_own, gin_near, gin_rest, both, held, sems):
    tokens, width = out_own.shape
    rows = tokens // NZ
    copies = []
    for k in range(NZ):
        back = (NZ - k) % NZ
        mine, theirs = pl.ds(k * rows, rows), pl.ds(back % 4 * rows, rows)
        for column, own, sent in (
            (0, out_own, out_near if back < 4 else out_rest),
            (width, gin_own, gin_near if back < 4 else gin_rest),
        ):
            total = own[mine, :].astype(f32) + sent[theirs, :].astype(f32)
            held[mine, pl.ds(column, width)] = total.astype(bf16)
        place = chunk_rows(chunk_at(s, k), rows)
        copy = pltpu.make_async_copy(held.at[mine], both.at[place], sems.at[k])
        copy.start()
        copies.append(copy)
    for copy in copies:
        copy.wait()


def total_kernel(s, *refs):
    parts, (out, gin) = refs[:-2], refs[-2:]
    rows, width = out.shape
    acc = jnp.zeros((rows, 2 * width), f32)
    for part in parts:
        for p in range(part.shape[0]):
            acc += part[p].astype(f32)
    out[...] = acc[:, :width].astype(bf16)
    gin[...] = acc[:, width:].astype(bf16)


def join_two_kernel(s, own, sent, out):
    units = own.shape[1]
    out[:, chunk_rows(s[CORE], units)] = own[...]
    out[:, chunk_rows(1 - s[CORE], units)] = sent[...]


def join_four_kernel(s, keep, core_sent, yl_sent, both_sent, out):
    quarter, units = keep.shape
    core, yl = s[CORE], s[YL]
    out[:, chunk_rows(2 * yl + core, units)] = keep[...]
    out[:, chunk_rows(2 * yl + 1 - core, units)] = core_sent[...]
    out[:, chunk_rows(2 * (1 - yl) + core, units)] = yl_sent[pl.ds(0, quarter), :]
    out[:, chunk_rows(2 * (1 - yl) + 1 - core, units)] = both_sent[...]


def on_device(inputs, cotangent, w_in, w_out):
    z, core, yl = lax.axis_index("z"), lax.axis_index("core"), lax.axis_index("yl")
    scalars = jnp.stack([z, core, yl, 2 * yl + core, 2 * yl + 1 - core]).astype(jnp.int32)
    rows, width = inputs.shape
    w_in, w_out = in_hbm(w_in), in_hbm(w_out)
    units = w_in.shape[1] // 4
    tokens = rows * NP
    chunk = tokens // NZ
    half = units // 2

    def w_in_block(which):
        return pl.BlockSpec((width, units), lambda i, s: (0, s[which]))

    def w_out_block(which):
        return pl.BlockSpec((units, width), lambda i, s: (s[which], 0))

    w_in_send, w_out_send, spread = call(
        prepare_kernel, scalars, (w_in, w_out, in_hbm(inputs), in_hbm(cotangent)),
        (w_in_block(THEIRS), w_out_block(THEIRS), None, None),
        [sds((width, units)), sds((units, width)), sds((tokens, 2 * width))],
    )
    own = plane_swap(spread)
    other = swap_core(own)
    w_in_other = swap_core(w_in_send)

    work = 4 * tokens * width * units
    partial_outs = [sds((tokens, units)), sds((chunk, half)), sds((chunk, half))]
    piece = sds((chunk, units))
    own_half, = call(
        own_half_kernel, scalars, (own, w_in), (None, w_in_block(MINE)), [sds((tokens, units))], work // 2,
    )
    first = call(
        other_half_kernel, scalars, (own_half, other, w_in_other), (None,) * 3, partial_outs, work // 2,
    )
    square = sds((2 * width, units))
    wi_turned, wo, wo_turned = call(
        arrange_kernel, scalars, (w_in, w_in_other, w_out, swap_core(w_out_send)),
        (w_in_block(MINE), None, w_out_block(MINE), None), [square] * 3, after=(first[1],),
    )
    second = call(
        partial_kernel, scalars, (own, other, wo_turned), (None,) * 3, partial_outs, work, after=(first[1],),
    )
    first = reduce_step(scalars, first, 3, (second[1],))
    second = reduce_step(scalars, second, 3, (first[1],))
    first = reduce_step(scalars, first, 2, (second[1],))
    second = reduce_step(scalars, second, 2, (first[1],))
    first = reduce_step(scalars, first, 1, (second[1],))
    second = reduce_step(scalars, second, 1, (first[1],))
    hidden_own, slope = call(
        hidden_kernel, scalars, last_terms(first), (None,) * 3,
        [piece, sds((chunk, units), f32)],
    )
    hidden_near = gather_near(hidden_own)
    hidden, hidden_far = gather_far(scalars, *hidden_near)
    grad_pre_own, = call(
        grad_pre_kernel, scalars, (*last_terms(second), slope), (None,) * 4, [piece],
        after=(hidden_own,),
    )

    grad_near = gather_near(grad_pre_own)
    grad_pre, far_send = gather_far(scalars, *grad_near)
    half_out, rest_out = sds((tokens, width)), sds((tokens // 2, width))
    quarter = pltpu.HBM((width // 2, units), bf16)
    keep, core_send, yl_send, hidden_all = call(
        w_out_kernel, scalars, (*hidden, own, other), (None,) * 11,
        [quarter, quarter, sds((width, units)), sds((tokens, units))], work,
        after=(far_send,),
    )
    yl_sent = lax.ppermute(yl_send, "yl", SWAP)
    core_sent = swap_core(core_send)
    out_own, *out_send = call(
        outputs_kernel, scalars, (hidden_all, wo), (None, None), [half_out, rest_out, rest_out], work, after=(yl_send, grad_pre[4], grad_pre[5]),
    )
    out_sent = [swap_core(half) for half in out_send]

    gin_own, gin_near, gin_rest, grad_pre_all = call(
        forward_kernel, scalars, (*grad_pre, wi_turned), (None,) * 10,
        [half_out, rest_out, rest_out, sds((tokens, units))], work, after=(out_send[0],),
    )
    both, = call(
        merge_kernel, scalars, (out_own, *out_sent, gin_own, swap_core(gin_near), swap_core(gin_rest)), (None,) * 6,
        [pltpu.HBM((tokens, 2 * width), bf16)], touched=0, after=(yl_sent,),
        out_specs=[pl.BlockSpec(memory_space=pl.ANY)],
        scratch=[pltpu.VMEM((tokens, 2 * width), bf16), pltpu.SemaphoreType.DMA((NZ,))],
    )
    parts = plane_swap(both).reshape(NP, rows, 2 * width)
    gwi_own, gwi_send = call(
        w_in_kernel, scalars, (grad_pre_all, own, other), (None,) * 3,
        [sds((width, units))] * 2, work,
    )
    both_sent = swap_core(yl_sent[width // 2:])
    grad_w_out, = call(
        join_four_kernel, scalars, (keep, core_sent, yl_sent, both_sent), (None,) * 4,
        [sds((width // 2, 4 * units))],
    )
    grad_w_in, = call(
        join_two_kernel, scalars, (gwi_own, swap_core(gwi_send)), (None, None),
        [sds((width, 2 * units))],
    )
    quarters = [
        pl.BlockSpec((NP // 4, rows, 2 * width), functools.partial(lambda q, i, s: (q, 0, 0), q)) for q in range(4)
    ]
    outputs, grad_inputs = call(total_kernel, scalars, (parts,) * 4, quarters, [sds((rows, width))] * 2)
    return outputs, grad_inputs, grad_w_in, grad_w_out.T


def solution(mesh):
    grid = Mesh(mesh.devices.reshape(NZ, 2, 2, 4, 2), ("z", "core", "yh", "x", "yl"))
    row, col = ("z", "core"), ("yh", "x")
    in_specs = (P(PLANE, row), P(PLANE, row), P(row, col), P(col, row))
    out_specs = (P(PLANE, row), P(PLANE, row), P(row, col + ("yl",)), P(col, row + ("yl",)))
    return jax.shard_map(
        on_device, mesh=grid, in_specs=in_specs, out_specs=out_specs, check_vma=False
    )
```
